32 devices in a mesh: lon: 8 (over z, core), lat: 4 (over y, x).
Axes of the slice: x: 2, y: 2, z: 4, core: 2. Of those that a mesh axis runs over, the one named last changes fastest.
Arguments:
- temp: float32 [8, 1024, 4096], P(None, 'lat', 'lon'), may hold values from -6 to 6
- currents: float32 [2, 8, 1024, 4096], P(None, None, 'lat', 'lon'), may hold values from -0.4 to 0.4
- mixing: float32 [7, 1024, 4096], P(None, 'lat', 'lon'), may hold values from 0.05 to 2
- ice_vel: float32 [2, 1024, 4096], P(None, 'lat', 'lon'), may hold values from -3 to 3
- strength: float32 [1024, 4096], P('lat', 'lon'), may hold values from 0.5 to 2
- ice_list: int32 [4, 8, 8], P('lat', 'lon'), may hold values from 0 to 8, as said below
- land: int32 [16, 16], P('lat', 'lon'), may hold values 0 or 1
Outputs:
- temp_out: float32 [8, 1024, 4096], P(None, 'lat', 'lon')
- ice_vel_out: float32 [2, 1024, 4096], P(None, 'lat', 'lon')
The draws below stay inside these ranges and needn't reach their ends.
Inputs may be any that keep to these rules, and one draw needn't show every extreme that they name: `ice_list`: each device's list holds distinct block numbers below 8, followed by entries equal to 8; the devices of one lat index list 4 * 8 blocks together, and some device of each lat index lists 8.
All inputs are finite; a program needn't handle non-finite values. No bound on the sum of `land` on one device may be relied on, other than what follows from the above.
Results may differ from the reference program's by a relative error of at most 0.00002.
Values sent between devices are 32-bit elements; how exact they have to be, the bound alone decides.
A program may use at most 128 MiB of HBM per device.

```python
import math
import jax
import jax.numpy as jnp
from jax import lax

CLAT = 256
CLON = 512
LEV = 8
CYCLES = 32
BLAT = 64
BLON = 256
NB = 8
OWN = 4
NLAT = 1024
NLON = 4096
NBLAT = 16
NBLON = 16
N_LON = 8
N_LAT = 4


def draw_ice_list(key, part):

    def one_row(row_key):
        first, second, third = jax.random.split(row_key, 3)
        order = jax.random.permutation(first, N_LON).astype(jnp.int32)
        places = jnp.argsort(order).astype(jnp.int32)
        shares = jax.random.randint(second, (N_LON // 2,), 0, OWN + 1).astype(jnp.int32)
        shares = shares.at[0].set(OWN)
        signs = 1 - 2 * (places % 2)
        counts = OWN + signs * shares[places // 2]
        device_keys = jax.random.split(third, N_LON)
        numbers = jax.vmap(lambda one_key: jax.random.permutation(one_key, NB).astype(jnp.int32))(device_keys)
        position = jnp.arange(NB, dtype=jnp.int32)
        return jnp.where(position[None, :] < counts[:, None], numbers, NB).astype(jnp.int32)
    return jax.vmap(one_row)(jax.random.split(key, N_LAT))


def place_ends(array, own_key, least, top_value):
    extent = array.shape
    index_at = [jax.random.randint(jax.random.fold_in(own_key, axis), (), 0, extent[axis]) for axis in range(len(extent))]
    array = array.at[tuple(index_at)].set(least)
    longest = extent.index(max(extent))
    index_at[longest] = (index_at[longest] + 1) % extent[longest]
    return array.at[tuple(index_at)].set(top_value)


def block_scale(rng, extent, pieces, low, top_value):
    def one(axis_at, blocks):
        draws = jax.random.uniform(jax.random.fold_in(jax.random.fold_in(rng, 6), axis_at), (blocks,), jnp.float32, low / len(pieces), top_value / len(pieces))
        return jnp.repeat(jnp.exp(draws), extent[axis_at] // blocks).reshape((-1,) + (1,) * (len(extent) - axis_at - 1))

    level = one(*pieces[0])
    for cut in pieces[1:]:
        level = level * one(*cut)
    return level


def bell_draw(stream_key, extent, scale, limit, cuts=(), kind=jnp.bfloat16):
    drawn = jax.random.normal(stream_key, extent, jnp.float32) * scale
    if len(cuts) > 0:
        drawn = block_scale(stream_key, extent, cuts, -0.22, 0.18) * drawn
    return jnp.clip(drawn, min=-limit, max=limit).astype(kind)


def setup_inputs(seed: int = 0) -> dict:
    key_list = jax.random.split(jax.random.key(seed), 8)
    temp = bell_draw(key_list[0], (LEV, NLAT, NLON), 1.0, 6.0, ((1, 4), (2, 8)), jnp.float32)
    currents = jnp.clip(jax.random.uniform(key_list[1], (2, LEV, NLAT, NLON), jnp.float32, -0.4, 0.4) * block_scale(key_list[1], (2, LEV, NLAT, NLON), ((2, 4), (3, 8)), -0.4, 0.0), -0.4, 0.4)
    mixing = jnp.clip(jnp.exp(math.log(2.0) - 3.6888794 * jax.random.uniform(key_list[2], (LEV - 1, NLAT, NLON), jnp.float32) ** block_scale(key_list[2], (LEV - 1, NLAT, NLON), ((1, 4), (2, 8)), -0.2, 0.2)), 0.05, 2.0)
    ice_vel = bell_draw(key_list[3], (2, NLAT, NLON), 0.5, 3.0, ((1, 4), (2, 8)), jnp.float32)
    strength = jnp.clip(jnp.exp(math.log(2.0) - 1.3862944 * jax.random.uniform(key_list[4], (NLAT, NLON), jnp.float32) ** block_scale(key_list[4], (NLAT, NLON), ((0, 4), (1, 8)), -0.2, 0.2)), 0.5, 2.0)
    ice_list = draw_ice_list(jax.random.fold_in(key_list[7], 71), 0)
    land = place_ends((jax.random.randint(key_list[6], (NBLAT, NBLON), 0, 4) < 1).astype(jnp.int32), jax.random.fold_in(key_list[6], 1), 0, 1)
    return dict(temp=temp, currents=currents, mixing=mixing, ice_vel=ice_vel, strength=strength, ice_list=ice_list, land=land)


diffusion_rate = 0.15
advect_rate = 0.5
relax_rate = 0.5
ice_step = 0.2
drag_rate = 1.0
strain_floor = 0.25
heat_rate = 0.5
freezing = -1.0

def east_diff(field):
    return jnp.concatenate([field[..., 1:] - field[..., :-1], jnp.zeros_like(field[..., :1])], axis=-1)

def north_diff(field):
    return jnp.concatenate([field[..., 1:, :] - field[..., :-1, :], jnp.zeros_like(field[..., :1, :])], axis=-2)

def west_diff(field):
    return jnp.concatenate([field[..., :1], field[..., 1:] - field[..., :-1]], axis=-1)

def south_diff(field):
    return jnp.concatenate([field[..., :1, :], field[..., 1:, :] - field[..., :-1, :]], axis=-2)

def subcycles(ice_u, ice_v, pressure, ocean_u, ocean_v, surface):

    def one_cycle(cycle, state):
        ice_u, ice_v, stress_one, stress_two = state
        diverge = east_diff(ice_u) + north_diff(ice_v)
        shearing = east_diff(ice_v) + north_diff(ice_u)
        delta = jnp.sqrt(diverge * diverge + shearing * shearing + strain_floor)
        viscous = pressure / (2.0 * delta)
        stress_one = (stress_one + relax_rate * (viscous * diverge - 0.5 * pressure)) / (1.0 + relax_rate)
        stress_two = (stress_two + relax_rate * viscous * shearing) / (1.0 + relax_rate)
        force_u = west_diff(stress_one) + south_diff(stress_two)
        force_v = south_diff(stress_one) + west_diff(stress_two)
        ice_u = (ice_u + ice_step * (force_u + drag_rate * ocean_u)) / (1.0 + ice_step * drag_rate)
        ice_v = (ice_v + ice_step * (force_v + drag_rate * ocean_v)) / (1.0 + ice_step * drag_rate)
        return (ice_u, ice_v, stress_one, stress_two)
    start = (ice_u, ice_v, jnp.zeros_like(ice_u), jnp.zeros_like(ice_u))
    ice_u, ice_v, stress_one, stress_two = lax.fori_loop(0, CYCLES, one_cycle, start)
    rel_u = ice_u - ocean_u
    rel_v = ice_v - ocean_v
    speed = jnp.sqrt(rel_u * rel_u + rel_v * rel_v + 0.01)
    return (ice_u, ice_v, heat_rate * speed * (freezing - surface))

def column_solve(right, mixing):
    levels = right.shape[0]
    ratios = []
    partial_value = []
    for level in range(levels):
        lower = mixing[level - 1] if level > 0 else 0.0
        upper = mixing[level] if level < levels - 1 else 0.0
        diagonal = 1.0 + lower + upper
        if level > 0:
            pivot = diagonal - lower * ratios[-1]
            value = (right[level] + lower * partial_value[-1]) / pivot
        else:
            pivot = diagonal + jnp.zeros_like(right[0])
            value = right[level] / pivot
        ratios.append(upper / pivot)
        partial_value.append(value)
    result = [partial_value[-1]]
    for level in range(levels - 2, -1, -1):
        result.insert(0, partial_value[level] + ratios[level] * result[0])
    return jnp.stack(result)

def to_blocks(field):
    lead = field.shape[:-2]
    rows, cols = field.shape[-2:]
    shaped = field.reshape(lead + (rows // BLAT, BLAT, cols // BLON, BLON))
    return jnp.moveaxis(shaped, -3, -2)

def from_blocks(blocks):
    lead = blocks.shape[:-4]
    shaped = jnp.moveaxis(blocks, -2, -3)
    sizes = blocks.shape[-4:]
    return shaped.reshape(lead + (sizes[0] * sizes[2], sizes[1] * sizes[3]))

def reference(temp, currents, mixing, ice_vel, strength, ice_list, land):
    rows_dev = CLAT // BLAT
    cols_dev = CLON // BLON
    numbers = jnp.arange(NB, dtype=jnp.int32)
    flags = jnp.any(ice_list[..., :, None] == numbers, axis=-2)
    flags = flags.reshape(N_LAT, N_LON, rows_dev, cols_dev).transpose(0, 2, 1, 3).reshape(NBLAT, NBLON)
    ice_cell = jnp.repeat(jnp.repeat(flags, BLAT, axis=0), BLON, axis=1)
    land_cell = jnp.repeat(jnp.repeat(land > 0, BLAT, axis=0), BLON, axis=1)
    fields = jnp.stack([ice_vel[0], ice_vel[1], strength, currents[0, 0], currents[1, 0], temp[0]])
    blocks = to_blocks(fields)
    new_u, new_v, flux = subcycles(blocks[0], blocks[1], blocks[2], blocks[3], blocks[4], blocks[5])
    new_u = from_blocks(new_u)
    new_v = from_blocks(new_v)
    flux = from_blocks(flux)
    ice_vel_out = jnp.where(ice_cell[None], jnp.stack([new_u, new_v]), ice_vel)
    east = jnp.roll(temp, -1, axis=2)
    west = jnp.roll(temp, 1, axis=2)
    north = jnp.concatenate([temp[:, 1:], jnp.flip(temp[:, -1:], axis=2)], axis=1)
    south = jnp.concatenate([temp[:, :1], temp[:, :-1]], axis=1)
    explicit = temp + diffusion_rate * (east + west + north + south - 4.0 * temp) - advect_rate * (currents[0] * (east - west) + currents[1] * (north - south))
    right = explicit.at[0].add(jnp.where(ice_cell, flux, jnp.float32(0.0)))
    solved = column_solve(right, mixing)
    temp_out = jnp.where(land_cell[None], temp, solved)
    return (temp_out, ice_vel_out)
```

```python
import functools

import jax
import jax.numpy as jnp
from jax import lax
from jax.experimental import pallas as pl
from jax.experimental.pallas import tpu as pltpu
from jax.sharding import PartitionSpec as P

CYCLES = 32
LANES = 128
SUBS = 8

diffusion_rate = 0.15
advect_rate = 0.5
relax_rate = 0.5
ice_step = 0.2
drag_rate = 1.0
strain_floor = 0.25
heat_rate = 0.5
freezing = -1.0

KEEP = 1.0 / (1.0 + ice_step * drag_rate)
GAIN = ice_step * KEEP
FADE = 1.0 / (1.0 + relax_rate)


def iota(dim):
    return lax.broadcasted_iota(jnp.int32, (SUBS, LANES), dim)


def ice_kernel(
    block_rows,
    block_cols,
    block_total,
    vel_hbm,
    strength_hbm,
    currents_hbm,
    temp_hbm,
    list_ref,
    vel_out,
    flux_out,
    nat,
    state,
    stress,
    fixed,
    sem_in,
    sem_out,
):
    pieces = nat.shape[1]
    group = state.shape[1]
    wide = block_cols // LANES
    per_block = block_rows // group
    cols_dev = pieces // wide
    fields = (
        vel_hbm.at[0],
        vel_hbm.at[1],
        strength_hbm,
        currents_hbm.at[0, 0],
        currents_hbm.at[1, 0],
        temp_hbm.at[0],
    )
    copies = []
    for f, field in enumerate(fields):
        for c in range(pieces):
            copy = pltpu.make_async_copy(
                field.at[:, pl.ds(c * LANES, LANES)], nat.at[f, c], sem_in.at[f, c]
            )
            copy.start()
            copies.append(copy)

    lane = iota(1)
    sub = iota(0)
    first_lane = lane == 0
    last_lane = lane == LANES - 1
    low_group = sub % per_block == 0
    high_group = sub % per_block == per_block - 1

    def strided(f, c, r):
        return nat[f, c, pl.ds(r, SUBS, stride=group), :]

    for copy in copies:
        copy.wait()

    def bring(r, carry):
        for c in range(pieces):
            state[0, r, c] = strided(0, c, r)
            state[1, r, c] = strided(1, c, r)
            fixed[0, r, c] = strided(2, c, r) * (GAIN * relax_rate * 0.5 * FADE)
            fixed[1, r, c] = strided(3, c, r) * (GAIN * drag_rate)
            fixed[2, r, c] = strided(4, c, r) * (GAIN * drag_rate)
            stress[0, r, c] = jnp.zeros((SUBS, LANES), jnp.float32)
            stress[1, r, c] = jnp.zeros((SUBS, LANES), jnp.float32)
        return carry

    lax.fori_loop(0, group, bring, 0)

    def east(row):
        result = []
        for c in range(pieces):
            if c % wide != wide - 1:
                result.append(
                    pltpu.roll(jnp.where(first_lane, row[c + 1], row[c]), LANES - 1, 1)
                )
            else:
                result.append(jnp.where(last_lane, row[c], pltpu.roll(row[c], LANES - 1, 1)))
        return result

    def west(row):
        result = []
        for c in range(pieces):
            if c % wide != 0:
                result.append(pltpu.roll(jnp.where(last_lane, row[c - 1], row[c]), 1, 1))
            else:
                result.append(jnp.where(first_lane, 0.0, pltpu.roll(row[c], 1, 1)))
        return result

    def read(ref, f, r):
        return [ref[f, r, c] for c in range(pieces)]

    def stresses(r, u, v, north_u, north_v):
        east_u = east(u)
        east_v = east(v)
        one = []
        two = []
        for c in range(pieces):
            both = u[c] + v[c]
            d = (east_u[c] + north_v[c]) - both
            h = (east_v[c] + north_u[c]) - both
            inverse = lax.rsqrt(d * d + h * h + strain_floor)
            q = fixed[0, r, c]
            w = q * inverse
            s_one = (FADE * stress[0, r, c] - q) + w * d
            s_two = FADE * stress[1, r, c] + w * h
            stress[0, r, c] = s_one
            stress[1, r, c] = s_two
            one.append(s_one)
            two.append(s_two)
        return one, two

    def moved(r, u, v, one, two, south_one, south_two):
        west_one = west(one)
        west_two = west(two)
        for c in range(pieces):
            both = one[c] + two[c]
            state[0, r, c] = (KEEP * u[c] + fixed[1, r, c]) + (
                both - (west_one[c] + south_two[c])
            )
            state[1, r, c] = (KEEP * v[c] + fixed[2, r, c]) + (
                both - (west_two[c] + south_one[c])
            )

    def one_cycle(cycle, carry):
        top = group - 1
        u = read(state, 0, 0)
        v = read(state, 1, 0)
        top_u = read(state, 0, top)
        top_v = read(state, 1, top)
        wrap_u = [
            jnp.where(high_group, t, pltpu.roll(x, SUBS - 1, 0)) for t, x in zip(top_u, u)
        ]
        wrap_v = [
            jnp.where(high_group, t, pltpu.roll(x, SUBS - 1, 0)) for t, x in zip(top_v, v)
        ]
        top_one, top_two = stresses(top, top_u, top_v, wrap_u, wrap_v)
        south_one = [jnp.where(low_group, 0.0, pltpu.roll(x, 1, 0)) for x in top_one]
        south_two = [jnp.where(low_group, 0.0, pltpu.roll(x, 1, 0)) for x in top_two]
        for r in range(top):
            if r + 1 < top:
                next_u = read(state, 0, r + 1)
                next_v = read(state, 1, r + 1)
            else:
                next_u, next_v = top_u, top_v
            one, two = stresses(r, u, v, next_u, next_v)
            moved(r, u, v, one, two, south_one, south_two)
            u, v, south_one, south_two = next_u, next_v, one, two
        moved(top, top_u, top_v, top_one, top_two, south_one, south_two)
        return carry

    lax.fori_loop(0, CYCLES, one_cycle, 0)

    entries = [list_ref[0, 0, i] for i in range(block_total)]
    masks = []
    for cb in range(cols_dev):
        mask = jnp.zeros((SUBS, LANES), jnp.int32)
        for rb in range(block_total // cols_dev):
            number = rb * cols_dev + cb
            hit = jnp.int32(0)
            for entry in entries:
                hit = jnp.where(entry == number, jnp.int32(1), hit)
            mask = jnp.where(sub // per_block == rb, hit, mask)
        masks.append(mask > 0)

    def finish(r, carry):
        for c in range(pieces):
            ice = masks[c // wide]
            u = state[0, r, c]
            v = state[1, r, c]
            rel_u = u - strided(3, c, r)
            rel_v = v - strided(4, c, r)
            speed = jnp.sqrt(rel_u * rel_u + rel_v * rel_v + 0.01)
            flux = heat_rate * speed * (freezing - strided(5, c, r))
            rows = pl.ds(r, SUBS, stride=group)
            nat[0, c, rows, :] = jnp.where(ice, u, strided(0, c, r))
            nat[1, c, rows, :] = jnp.where(ice, v, strided(1, c, r))
            nat[5, c, rows, :] = jnp.where(ice, flux, 0.0)
        return carry

    lax.fori_loop(0, group, finish, 0)
    copies = []
    for k, (f, target) in enumerate(((0, vel_out.at[0]), (1, vel_out.at[1]), (5, flux_out))):
        for c in range(pieces):
            copy = pltpu.make_async_copy(
                nat.at[f, c], target.at[:, pl.ds(c * LANES, LANES)], sem_out.at[k, c]
            )
            copy.start()
            copies.append(copy)
    for copy in copies:
        copy.wait()


def ice_step_call(ice_vel, strength, currents, temp, ice_list, block_rows, block_cols):
    rows, cols = strength.shape
    pieces = cols // LANES
    group = rows // SUBS
    block_total = ice_list.shape[-1]
    anywhere = pl.BlockSpec(memory_space=pl.ANY)
    lay = (group, pieces, SUBS, LANES)
    return pl.pallas_call(
        functools.partial(ice_kernel, block_rows, block_cols, block_total),
        out_shape=(
            jax.ShapeDtypeStruct(ice_vel.shape, jnp.float32),
            jax.ShapeDtypeStruct(strength.shape, jnp.float32),
        ),
        in_specs=[anywhere] * 4 + [pl.BlockSpec(memory_space=pltpu.SMEM)],
        out_specs=(anywhere, anywhere),
        scratch_shapes=[
            pltpu.VMEM((6, pieces, rows, LANES), jnp.float32),
            pltpu.VMEM((2,) + lay, jnp.float32),
            pltpu.VMEM((2,) + lay, jnp.float32),
            pltpu.VMEM((3,) + lay, jnp.float32),
            pltpu.SemaphoreType.DMA((6, pieces)),
            pltpu.SemaphoreType.DMA((3, pieces)),
        ],
        cost_estimate=pl.CostEstimate(
            flops=CYCLES * 40 * rows * cols,
            bytes_accessed=9 * 4 * rows * cols,
            transcendentals=CYCLES * rows * cols,
        ),
        compiler_params=pltpu.CompilerParams(vmem_limit_bytes=16 * 2**20),
        name="ice_subcycles",
    )(ice_vel, strength, currents, temp, ice_list)


STRIP = 16


def ocean_kernel(
    block_rows,
    block_cols,
    chunk,
    temp_hbm,
    currents_hbm,
    mixing_hbm,
    flux_hbm,
    west_ref,
    east_ref,
    south_ref,
    north_ref,
    mirror_ref,
    land_ref,
    out_hbm,
    temp,
    currents,
    mixing,
    flux,
    out,
    sem_in,
    sem_out,
):
    levels, held_rows, cols = temp.shape
    rows = held_rows - 2 * SUBS
    pieces = cols // LANES
    chunks = rows // chunk
    wide = block_cols // LANES
    lat_index = lax.axis_index("lat")
    lat_count = lax.axis_size("lat")

    def incoming(i):
        span = pl.ds(i * chunk, chunk)
        return (
            pltpu.make_async_copy(
                temp_hbm.at[:, span],
                temp.at[:, pl.ds(SUBS + i * chunk, chunk)],
                sem_in.at[0, i],
            ),
            pltpu.make_async_copy(
                currents_hbm.at[:, :, span], currents.at[:, :, span], sem_in.at[1, i]
            ),
            pltpu.make_async_copy(mixing_hbm.at[:, span], mixing.at[:, span], sem_in.at[2, i]),
            pltpu.make_async_copy(flux_hbm.at[span], flux.at[span], sem_in.at[3, i]),
        )

    def outgoing(i):
        span = pl.ds(i * chunk, chunk)
        return pltpu.make_async_copy(out.at[:, span], out_hbm.at[:, span], sem_out.at[i])

    for i in range(chunks):
        for copy in incoming(i):
            copy.start()

    lane = lax.broadcasted_iota(jnp.int32, (STRIP, LANES), 1)
    sub = lax.broadcasted_iota(jnp.int32, (STRIP, LANES), 0)
    first_lane = lane == 0
    last_lane = lane == LANES - 1
    low_sub = sub == 0
    high_sub = sub == STRIP - 1

    swap = (
        lax.broadcasted_iota(jnp.int32, (LANES, LANES), 0)
        + lax.broadcasted_iota(jnp.int32, (LANES, LANES), 1)
        == LANES - 1
    ).astype(jnp.float32)
    at_top = lat_index == lat_count - 1
    west_cols = jnp.transpose(west_ref[...])
    east_cols = jnp.transpose(east_ref[...])

    incoming(0)[0].wait()
    for c in range(pieces):
        span = pl.ds(c * LANES, LANES)
        across = pl.ds((pieces - 1 - c) * LANES, LANES)
        flipped = jnp.dot(
            mirror_ref[:, across],
            swap,
            precision=lax.Precision.HIGHEST,
            preferred_element_type=jnp.float32,
        )
        north = jnp.where(at_top, flipped, north_ref[:, span])
        for k in range(levels):
            temp[k, pl.ds(0, SUBS), span] = jnp.where(
                lat_index == 0,
                jnp.broadcast_to(temp[k, SUBS : SUBS + 1, span], (SUBS, LANES)),
                jnp.broadcast_to(south_ref[k : k + 1, span], (SUBS, LANES)),
            )
            temp[k, pl.ds(SUBS + rows, SUBS), span] = jnp.broadcast_to(
                north[k : k + 1], (SUBS, LANES)
            )

    for i in range(chunks):
        if i + 1 < chunks:
            incoming(i + 1)[0].wait()
        for copy in incoming(i)[1:]:
            copy.wait()
        for s in range(chunk // STRIP):
            base = i * chunk + s * STRIP
            span = pl.ds(base, STRIP)
            for c in range(pieces):
                here = pl.ds(c * LANES, LANES)
                right = []
                for k in range(levels):
                    mid = temp[k, pl.ds(SUBS + base, STRIP), here]
                    below = temp[k, pl.ds(base, SUBS), here]
                    above = temp[k, pl.ds(SUBS + base + STRIP, SUBS), here]
                    if c + 1 < pieces:
                        beyond = temp[
                            k, pl.ds(SUBS + base, STRIP), pl.ds((c + 1) * LANES, LANES)
                        ]
                    else:
                        beyond = east_cols[base : base + STRIP, k : k + 1]
                    if c > 0:
                        before = temp[
                            k, pl.ds(SUBS + base, STRIP), pl.ds((c - 1) * LANES, LANES)
                        ]
                    else:
                        before = west_cols[base : base + STRIP, k : k + 1]
                    east = pltpu.roll(jnp.where(first_lane, beyond, mid), LANES - 1, 1)
                    west = pltpu.roll(jnp.where(last_lane, before, mid), 1, 1)
                    above = jnp.concatenate([above] * (STRIP // SUBS), axis=0)
                    below = jnp.concatenate([below] * (STRIP // SUBS), axis=0)
                    north = pltpu.roll(jnp.where(low_sub, above, mid), STRIP - 1, 0)
                    south = pltpu.roll(jnp.where(high_sub, below, mid), 1, 0)
                    flow = currents[0, k, span, here] * (east - west) + currents[
                        1, k, span, here
                    ] * (north - south)
                    value = (
                        (1.0 - 4.0 * diffusion_rate) * mid
                        + diffusion_rate * ((east + west) + (north + south))
                    ) - advect_rate * flow
                    if k == 0:
                        value = value + flux[span, here]
                    right.append(value)
                ahead = jnp.ones((STRIP, LANES), jnp.float32)
                tail = None
                weights = [None] * levels
                lifts = [None] * levels
                whole = [None] * levels
                gathered = None
                for k in range(levels - 1, -1, -1):
                    if k == levels - 1:
                        tail = ahead
                        gathered = right[k]
                    else:
                        a = mixing[k, span, here]
                        tail = ahead + a * tail
                        gathered = right[k] * ahead + a * gathered
                    if k > 0:
                        lifts[k] = mixing[k - 1, span, here] * ahead
                        ahead = tail + lifts[k]
                    else:
                        ahead = tail
                    whole[k] = gathered
                    weights[k] = 1.0 / ahead
                is_land = land_ref[base // block_rows, c // wide] > 0
                x = None
                for k in range(levels):
                    x = (whole[k] if k == 0 else whole[k] + lifts[k] * x) * weights[k]
                    out[k, span, here] = jnp.where(
                        is_land, temp[k, pl.ds(SUBS + base, STRIP), here], x
                    )
        outgoing(i).start()
    for i in range(chunks):
        outgoing(i).wait()


def ocean_call(temp, currents, mixing, flux, edges, land, block_rows, block_cols):
    levels, rows, cols = temp.shape
    chunk = min(32, block_rows)
    anywhere = pl.BlockSpec(memory_space=pl.ANY)
    inside = pl.BlockSpec(memory_space=pltpu.VMEM)
    return pl.pallas_call(
        functools.partial(ocean_kernel, block_rows, block_cols, chunk),
        out_shape=jax.ShapeDtypeStruct(temp.shape, jnp.float32),
        in_specs=[anywhere] * 4 + [inside] * 5 + [pl.BlockSpec(memory_space=pltpu.SMEM)],
        out_specs=anywhere,
        scratch_shapes=[
            pltpu.VMEM((levels, rows + 2 * SUBS, cols), jnp.float32),
            pltpu.VMEM(currents.shape, jnp.float32),
            pltpu.VMEM(mixing.shape, jnp.float32),
            pltpu.VMEM(flux.shape, jnp.float32),
            pltpu.VMEM(temp.shape, jnp.float32),
            pltpu.SemaphoreType.DMA((4, rows // chunk)),
            pltpu.SemaphoreType.DMA((rows // chunk,)),
        ],
        cost_estimate=pl.CostEstimate(
            flops=45 * levels * rows * cols,
            bytes_accessed=5 * 4 * levels * rows * cols,
            transcendentals=levels * rows * cols,
        ),
        compiler_params=pltpu.CompilerParams(vmem_limit_bytes=40 * 2**20),
        name="ocean_column",
    )(temp, currents, mixing, flux, *edges, land)


def shards(temp, currents, mixing, ice_vel, strength, ice_list, land):
    levels, rows, cols = temp.shape
    lat_count = lax.axis_size("lat")
    lon_count = lax.axis_size("lon")
    block_rows = 2 * rows // lon_count
    block_cols = cols // 2
    up = [(i, (i + 1) % lon_count) for i in range(lon_count)]
    down = [(target, source) for source, target in up]
    north_up = [(i, i + 1) for i in range(lat_count - 1)]
    south_down = [(target, source) for source, target in north_up]
    across = [(i, lon_count - 1 - i) for i in range(lon_count)]
    from_west = lax.ppermute(temp[:, :, -1], "lon", up)
    from_east = lax.ppermute(temp[:, :, 0], "lon", down)
    top_row = temp[:, -1, :]
    from_south = lax.ppermute(top_row, "lat", north_up)
    from_north = lax.ppermute(temp[:, 0, :], "lat", south_down)
    mirrored = lax.ppermute(top_row, "lon", across)
    vel_out, flux = ice_step_call(
        ice_vel, strength, currents, temp, ice_list, block_rows, block_cols
    )
    temp_out = ocean_call(
        temp,
        currents,
        mixing,
        flux,
        (from_west, from_east, from_south, from_north, mirrored),
        land,
        block_rows,
        block_cols,
    )
    return (temp_out, vel_out)


def solution(mesh):
    placed = (
        P(None, "lat", "lon"),
        P(None, None, "lat", "lon"),
        P(None, "lat", "lon"),
        P(None, "lat", "lon"),
        P("lat", "lon"),
        P("lat", "lon", None),
        P("lat", "lon"),
    )
    return jax.shard_map(
        shards,
        mesh=mesh,
        in_specs=placed,
        out_specs=(P(None, "lat", "lon"), P(None, "lat", "lon")),
        check_vma=False,
    )
```

```python
import functools

import jax
import jax.numpy as jnp
from jax import lax
from jax.experimental import pallas as pl
from jax.experimental.pallas import tpu as pltpu
from jax.sharding import PartitionSpec as P

CYCLES = 32
LANES = 128
SUBS = 8

diffusion_rate = 0.15
advect_rate = 0.5
relax_rate = 0.5
ice_step = 0.2
drag_rate = 1.0
strain_floor = 0.25
heat_rate = 0.5
freezing = -1.0

KEEP = 1.0 / (1.0 + ice_step * drag_rate)
GAIN = ice_step * KEEP
FADE = 1.0 / (1.0 + relax_rate)


def iota(dim):
    return lax.broadcasted_iota(jnp.int32, (SUBS, LANES), dim)


def exact_dot(value, picks):
    high = value.astype(jnp.bfloat16)
    rest = value - high.astype(jnp.float32)
    middle = rest.astype(jnp.bfloat16)
    low = (rest - middle.astype(jnp.float32)).astype(jnp.bfloat16)
    total = jnp.dot(low, picks, preferred_element_type=jnp.float32)
    total = total + jnp.dot(middle, picks, preferred_element_type=jnp.float32)
    return total + jnp.dot(high, picks, preferred_element_type=jnp.float32)


def edge_kernel(
    temp_hbm,
    west_out,
    east_out,
    south_out,
    north_out,
    mirror_out,
    columns,
    edge_rows,
    packed,
    low_row,
    high_row,
    landed_cols,
    landed_rows,
    sem_in,
    sem_send,
    sem_recv,
):
    levels, rows, cols = temp_hbm.shape
    lat = lax.axis_index("lat")
    lon = lax.axis_index("lon")
    lat_count = lax.axis_size("lat")
    lon_count = lax.axis_size("lon")
    west = {"lon": lax.rem(lon + lon_count - 1, lon_count)}
    east = {"lon": lax.rem(lon + 1, lon_count)}
    south = {"lat": lax.rem(lat + lat_count - 1, lat_count)}
    north = {"lat": lax.rem(lat + 1, lat_count)}
    mirror = {"lon": lon_count - 1 - lon}
    barrier = pltpu.get_barrier_semaphore()
    partners = (west, east, south, north, mirror)
    for partner in partners:
        pl.semaphore_signal(
            barrier, inc=1, device_id=partner, device_id_type=pl.DeviceIdType.MESH
        )
    row_copies = [
        pltpu.make_async_copy(temp_hbm.at[:, pl.ds(0, SUBS)], edge_rows.at[0], sem_in.at[0]),
        pltpu.make_async_copy(
            temp_hbm.at[:, pl.ds(rows - SUBS, SUBS)], edge_rows.at[1], sem_in.at[1]
        ),
    ]
    col_copies = [
        pltpu.make_async_copy(temp_hbm.at[:, :, pl.ds(0, LANES)], columns.at[0], sem_in.at[2]),
        pltpu.make_async_copy(
            temp_hbm.at[:, :, pl.ds(cols - LANES, LANES)], columns.at[1], sem_in.at[3]
        ),
    ]
    for copy in row_copies + col_copies:
        copy.start()
    for copy in row_copies:
        copy.wait()
    for k in range(levels):
        low_row[k : k + 1, :] = edge_rows[0, k, 0:1, :]
        high_row[k : k + 1, :] = edge_rows[1, k, SUBS - 1 : SUBS, :]
    pl.semaphore_wait(barrier, len(partners))

    def send(slot, source, target, partner):
        copy = pltpu.make_async_remote_copy(
            src_ref=source,
            dst_ref=target,
            send_sem=sem_send.at[slot],
            recv_sem=sem_recv.at[slot],
            device_id=partner,
            device_id_type=pl.DeviceIdType.MESH,
        )
        copy.start()
        return copy

    sent = [
        send(0, high_row, landed_rows.at[0], north),
        send(1, low_row, landed_rows.at[1], south),
        send(2, high_row, landed_rows.at[2], mirror),
    ]
    from_lane = lax.broadcasted_iota(jnp.int32, (LANES, LANES), 0)
    to_lane = lax.broadcasted_iota(jnp.int32, (LANES, LANES), 1)
    for copy in col_copies:
        copy.wait()
    total = jnp.zeros((rows, LANES), jnp.float32)
    for side, lane in ((0, 0), (1, LANES - 1)):
        for k in range(levels):
            picks = (from_lane == lane) & (to_lane == side * levels + k)
            total = total + exact_dot(
                columns[side, k], picks.astype(jnp.float32).astype(jnp.bfloat16)
            )
    packed[...] = total
    sent.append(send(3, packed, landed_cols.at[0], east))
    sent.append(send(4, packed, landed_cols.at[1], west))
    for copy in sent:
        copy.wait()
    west_out[...] = landed_cols[0]
    east_out[...] = landed_cols[1]
    south_out[...] = landed_rows[0]
    north_out[...] = landed_rows[1]
    mirror_out[...] = landed_rows[2]


def edges_call(temp):
    levels, rows, cols = temp.shape
    inside = pl.BlockSpec(memory_space=pltpu.VMEM)
    side = jax.ShapeDtypeStruct((rows, LANES), jnp.float32)
    line = jax.ShapeDtypeStruct((levels, cols), jnp.float32)
    return pl.pallas_call(
        edge_kernel,
        out_shape=(side, side, line, line, line),
        in_specs=[pl.BlockSpec(memory_space=pl.ANY)],
        out_specs=(inside,) * 5,
        scratch_shapes=[
            pltpu.VMEM((2, levels, rows, LANES), jnp.float32),
            pltpu.VMEM((2, levels, SUBS, cols), jnp.float32),
            pltpu.VMEM((rows, LANES), jnp.float32),
            pltpu.VMEM((levels, cols), jnp.float32),
            pltpu.VMEM((levels, cols), jnp.float32),
            pltpu.VMEM((2, rows, LANES), jnp.float32),
            pltpu.VMEM((3, levels, cols), jnp.float32),
            pltpu.SemaphoreType.DMA((4,)),
            pltpu.SemaphoreType.DMA((5,)),
            pltpu.SemaphoreType.DMA((5,)),
        ],
        compiler_params=pltpu.CompilerParams(
            collective_id=0, has_side_effects=True, vmem_limit_bytes=56 * 2**20
        ),
        name="edge_exchange",
    )(temp)


def ice_kernel(
    block_rows,
    block_cols,
    block_total,
    vel_hbm,
    strength_hbm,
    currents_hbm,
    temp_hbm,
    list_ref,
    vel_out,
    flux_out,
    raw,
    spread,
    state_a,
    state_b,
    stress_a,
    stress_b,
    fixed,
    sem_in,
    sem_out,
):
    rows, cols = raw.shape[1:]
    group, pieces = state_a.shape[1:3]
    per_block = block_rows // group
    lanes_block = block_cols // pieces
    cols_dev = cols // block_cols
    fields = (
        vel_hbm.at[0],
        vel_hbm.at[1],
        strength_hbm,
        currents_hbm.at[0, 0],
        currents_hbm.at[1, 0],
        temp_hbm.at[0],
    )
    copies = [
        pltpu.make_async_copy(field, raw.at[f], sem_in.at[f]) for f, field in enumerate(fields)
    ]
    for copy in copies:
        copy.start()

    lane = iota(1)
    sub = iota(0)
    first_lane = lane % lanes_block == 0
    last_lane = lane % lanes_block == lanes_block - 1
    low_group = sub % per_block == 0
    high_group = sub % per_block == per_block - 1

    def picks(dim):
        near = lax.broadcasted_iota(jnp.int32, (cols, cols), dim)
        far = lax.broadcasted_iota(jnp.int32, (cols, cols), 1 - dim)
        return (near == pieces * (far % LANES) + far // LANES).astype(jnp.float32).astype(
            jnp.bfloat16
        )

    to_pieces = picks(0)
    factors = (
        1.0,
        1.0,
        GAIN * relax_rate * 0.5 * FADE,
        GAIN * drag_rate,
        GAIN * drag_rate,
    )
    targets = (
        state_a.at[0],
        state_a.at[1],
        fixed.at[0],
        fixed.at[1],
        fixed.at[2],
    )
    for f in range(5):
        copies[f].wait()
        moved_cols = exact_dot(raw[f], to_pieces)
        for c in range(pieces):
            spread[f, c] = moved_cols[:, c * LANES : (c + 1) * LANES]
    copies[5].wait()

    def bring(r, carry):
        for f in range(5):
            for c in range(pieces):
                value = spread[f, c, pl.ds(r, SUBS, stride=group), :]
                targets[f][r, c] = value if f < 2 else value * factors[f]
        for c in range(pieces):
            stress_a[0, r, c] = jnp.zeros((SUBS, LANES), jnp.float32)
            stress_a[1, r, c] = jnp.zeros((SUBS, LANES), jnp.float32)
        return carry

    lax.fori_loop(0, group, bring, 0)

    def east(row):
        around = jnp.where(last_lane, row[-1], pltpu.roll(row[0], LANES - 1, 1))
        return row[1:] + [around]

    def west(row):
        around = jnp.where(first_lane, 0.0, pltpu.roll(row[-1], 1, 1))
        return [around] + row[:-1]

    def read(ref, f, r):
        return [ref[f, r, c] for c in range(pieces)]

    def one_cycle(state, stress, state_to, stress_to):
        def stresses(r, u, v, north_u, north_v):
            east_u = east(u)
            east_v = east(v)
            one = []
            two = []
            for c in range(pieces):
                both = u[c] + v[c]
                d = (east_u[c] + north_v[c]) - both
                h = (east_v[c] + north_u[c]) - both
                inverse = lax.rsqrt(d * d + h * h + strain_floor)
                q = fixed[0, r, c]
                w = q * inverse
                s_one = (FADE * stress[0, r, c] - q) + w * d
                s_two = FADE * stress[1, r, c] + w * h
                stress_to[0, r, c] = s_one
                stress_to[1, r, c] = s_two
                one.append(s_one)
                two.append(s_two)
            return one, two

        def moved(r, u, v, one, two, south_one, south_two):
            west_one = west(one)
            west_two = west(two)
            for c in range(pieces):
                both = one[c] + two[c]
                state_to[0, r, c] = (KEEP * u[c] + fixed[1, r, c]) + (
                    both - (west_one[c] + south_two[c])
                )
                state_to[1, r, c] = (KEEP * v[c] + fixed[2, r, c]) + (
                    both - (west_two[c] + south_one[c])
                )

        top = group - 1
        u = read(state, 0, 0)
        v = read(state, 1, 0)
        top_u = read(state, 0, top)
        top_v = read(state, 1, top)
        wrap_u = [
            jnp.where(high_group, t, pltpu.roll(x, SUBS - 1, 0)) for t, x in zip(top_u, u)
        ]
        wrap_v = [
            jnp.where(high_group, t, pltpu.roll(x, SUBS - 1, 0)) for t, x in zip(top_v, v)
        ]
        top_one, top_two = stresses(top, top_u, top_v, wrap_u, wrap_v)
        south_one = [jnp.where(low_group, 0.0, pltpu.roll(x, 1, 0)) for x in top_one]
        south_two = [jnp.where(low_group, 0.0, pltpu.roll(x, 1, 0)) for x in top_two]
        for r in range(group):
            if r < top:
                next_u = read(state, 0, r + 1)
                next_v = read(state, 1, r + 1)
                one, two = stresses(r, u, v, next_u, next_v)
            else:
                one = read(stress_to, 0, top)
                two = read(stress_to, 1, top)
            moved(r, u, v, one, two, south_one, south_two)
            u, v, south_one, south_two = next_u, next_v, one, two

    def two_cycles(cycle, carry):
        one_cycle(state_a, stress_a, state_b, stress_b)
        one_cycle(state_b, stress_b, state_a, stress_a)
        return carry

    lax.fori_loop(0, CYCLES // 2, two_cycles, 0)

    def put(r, carry):
        for f in range(2):
            for c in range(pieces):
                spread[f, c, pl.ds(r, SUBS, stride=group), :] = state_a[f, r, c]
        return carry

    lax.fori_loop(0, group, put, 0)

    entries = [list_ref[0, 0, i] for i in range(block_total)]
    from_pieces = picks(1)
    new_u, new_v = (
        exact_dot(
            jnp.concatenate([spread[f, c] for c in range(pieces)], axis=1), from_pieces
        )
        for f in range(2)
    )
    spread_u = new_u
    spread_v = new_v
    for number in range(block_total):
        hit = jnp.int32(0)
        for entry in entries:
            hit = jnp.where(entry == number, jnp.int32(1), hit)
        ice = hit > 0
        low = number // cols_dev * block_rows
        left = number % cols_dev * block_cols
        here = (slice(low, low + block_rows), slice(left, left + block_cols))
        u = spread_u[here]
        v = spread_v[here]
        rel_u = u - raw[(3,) + here]
        rel_v = v - raw[(4,) + here]
        speed = jnp.sqrt(rel_u * rel_u + rel_v * rel_v + 0.01)
        flux = heat_rate * speed * (freezing - raw[(5,) + here])
        raw[(0,) + here] = jnp.where(ice, u, raw[(0,) + here])
        raw[(1,) + here] = jnp.where(ice, v, raw[(1,) + here])
        raw[(5,) + here] = jnp.where(ice, flux, 0.0)
    copies = []
    for k, (f, target) in enumerate(((0, vel_out.at[0]), (1, vel_out.at[1]), (5, flux_out))):
        copy = pltpu.make_async_copy(raw.at[f], target, sem_out.at[k])
        copy.start()
        copies.append(copy)
    for copy in copies:
        copy.wait()


def ice_step_call(ice_vel, strength, currents, temp, ice_list, block_rows, block_cols):
    rows, cols = strength.shape
    pieces = cols // LANES
    group = rows // SUBS
    block_total = ice_list.shape[-1]
    anywhere = pl.BlockSpec(memory_space=pl.ANY)
    lay = (group, pieces, SUBS, LANES)
    return pl.pallas_call(
        functools.partial(ice_kernel, block_rows, block_cols, block_total),
        out_shape=(
            jax.ShapeDtypeStruct(ice_vel.shape, jnp.float32),
            jax.ShapeDtypeStruct(strength.shape, jnp.float32),
        ),
        in_specs=[anywhere] * 4 + [pl.BlockSpec(memory_space=pltpu.SMEM)],
        out_specs=(anywhere, anywhere),
        scratch_shapes=[
            pltpu.VMEM((6, rows, cols), jnp.float32),
            pltpu.VMEM((5, pieces, rows, LANES), jnp.float32),
            pltpu.VMEM((2,) + lay, jnp.float32),
            pltpu.VMEM((2,) + lay, jnp.float32),
            pltpu.VMEM((2,) + lay, jnp.float32),
            pltpu.VMEM((2,) + lay, jnp.float32),
            pltpu.VMEM((3,) + lay, jnp.float32),
            pltpu.SemaphoreType.DMA((6,)),
            pltpu.SemaphoreType.DMA((3,)),
        ],
        cost_estimate=pl.CostEstimate(
            flops=CYCLES * 40 * rows * cols,
            bytes_accessed=9 * 4 * rows * cols,
            transcendentals=CYCLES * rows * cols,
        ),
        compiler_params=pltpu.CompilerParams(vmem_limit_bytes=56 * 2**20),
        name="ice_subcycles",
    )(ice_vel, strength, currents, temp, ice_list)


STRIP = 16


def ocean_kernel(
    block_rows,
    block_cols,
    chunk,
    temp_hbm,
    currents_hbm,
    mixing_hbm,
    flux_hbm,
    west_ref,
    east_ref,
    south_ref,
    north_ref,
    mirror_ref,
    land_ref,
    out_hbm,
    temp,
    currents,
    mixing,
    flux,
    out,
    sem_in,
    sem_out,
):
    levels, held_rows, cols = temp.shape
    rows = held_rows - 2 * SUBS
    pieces = cols // LANES
    chunks = rows // chunk
    wide = block_cols // LANES
    lat_index = lax.axis_index("lat")
    lat_count = lax.axis_size("lat")

    def incoming(i):
        span = pl.ds(i * chunk, chunk)
        return (
            pltpu.make_async_copy(
                temp_hbm.at[:, span],
                temp.at[:, pl.ds(SUBS + i * chunk, chunk)],
                sem_in.at[0, i],
            ),
            pltpu.make_async_copy(
                currents_hbm.at[:, :, span], currents.at[:, :, span], sem_in.at[1, i]
            ),
            pltpu.make_async_copy(mixing_hbm.at[:, span], mixing.at[:, span], sem_in.at[2, i]),
            pltpu.make_async_copy(flux_hbm.at[span], flux.at[span], sem_in.at[3, i]),
        )

    def outgoing(i):
        span = pl.ds(i * chunk, chunk)
        return pltpu.make_async_copy(out.at[:, span], out_hbm.at[:, span], sem_out.at[i])

    for i in range(chunks):
        for copy in incoming(i):
            copy.start()

    lane = lax.broadcasted_iota(jnp.int32, (STRIP, LANES), 1)
    sub = lax.broadcasted_iota(jnp.int32, (STRIP, LANES), 0)
    first_lane = lane == 0
    last_lane = lane == LANES - 1
    low_sub = sub == 0
    high_sub = sub == STRIP - 1

    swap = (
        lax.broadcasted_iota(jnp.int32, (LANES, LANES), 0)
        + lax.broadcasted_iota(jnp.int32, (LANES, LANES), 1)
        == LANES - 1
    ).astype(jnp.float32)
    at_top = lat_index == lat_count - 1

    incoming(0)[0].wait()
    for c in range(pieces):
        span = pl.ds(c * LANES, LANES)
        across = pl.ds((pieces - 1 - c) * LANES, LANES)
        flipped = jnp.dot(
            mirror_ref[:, across],
            swap,
            precision=lax.Precision.HIGHEST,
            preferred_element_type=jnp.float32,
        )
        north = jnp.where(at_top, flipped, north_ref[:, span])
        for k in range(levels):
            temp[k, pl.ds(0, SUBS), span] = jnp.where(
                lat_index == 0,
                jnp.broadcast_to(temp[k, SUBS : SUBS + 1, span], (SUBS, LANES)),
                jnp.broadcast_to(south_ref[k : k + 1, span], (SUBS, LANES)),
            )
            temp[k, pl.ds(SUBS + rows, SUBS), span] = jnp.broadcast_to(
                north[k : k + 1], (SUBS, LANES)
            )

    for i in range(chunks):
        if i + 1 < chunks:
            incoming(i + 1)[0].wait()
        for copy in incoming(i)[1:]:
            copy.wait()
        for s in range(chunk // STRIP):
            base = i * chunk + s * STRIP
            span = pl.ds(base, STRIP)
            for c in range(pieces):
                here = pl.ds(c * LANES, LANES)
                right = []
                for k in range(levels):
                    mid = temp[k, pl.ds(SUBS + base, STRIP), here]
                    below = temp[k, pl.ds(base, SUBS), here]
                    above = temp[k, pl.ds(SUBS + base + STRIP, SUBS), here]
                    if c + 1 < pieces:
                        beyond = temp[
                            k, pl.ds(SUBS + base, STRIP), pl.ds((c + 1) * LANES, LANES)
                        ]
                    else:
                        beyond = east_ref[base : base + STRIP, k : k + 1]
                    if c > 0:
                        before = temp[
                            k, pl.ds(SUBS + base, STRIP), pl.ds((c - 1) * LANES, LANES)
                        ]
                    else:
                        before = west_ref[
                            base : base + STRIP, levels + k : levels + k + 1
                        ]
                    east = pltpu.roll(jnp.where(first_lane, beyond, mid), LANES - 1, 1)
                    west = pltpu.roll(jnp.where(last_lane, before, mid), 1, 1)
                    above = jnp.concatenate([above] * (STRIP // SUBS), axis=0)
                    below = jnp.concatenate([below] * (STRIP // SUBS), axis=0)
                    north = pltpu.roll(jnp.where(low_sub, above, mid), STRIP - 1, 0)
                    south = pltpu.roll(jnp.where(high_sub, below, mid), 1, 0)
                    flow = currents[0, k, span, here] * (east - west) + currents[
                        1, k, span, here
                    ] * (north - south)
                    value = (
                        (1.0 - 4.0 * diffusion_rate) * mid
                        + diffusion_rate * ((east + west) + (north + south))
                    ) - advect_rate * flow
                    if k == 0:
                        value = value + flux[span, here]
                    right.append(value)
                ahead = jnp.ones((STRIP, LANES), jnp.float32)
                tail = None
                weights = [None] * levels
                lifts = [None] * levels
                whole = [None] * levels
                gathered = None
                for k in range(levels - 1, -1, -1):
                    if k == levels - 1:
                        tail = ahead
                        gathered = right[k]
                    else:
                        a = mixing[k, span, here]
                        tail = ahead + a * tail
                        gathered = right[k] * ahead + a * gathered
                    if k > 0:
                        lifts[k] = mixing[k - 1, span, here] * ahead
                        ahead = tail + lifts[k]
                    else:
                        ahead = tail
                    whole[k] = gathered
                    weights[k] = 1.0 / ahead
                is_land = land_ref[base // block_rows, c // wide] > 0
                x = None
                for k in range(levels):
                    x = (whole[k] if k == 0 else whole[k] + lifts[k] * x) * weights[k]
                    out[k, span, here] = jnp.where(
                        is_land, temp[k, pl.ds(SUBS + base, STRIP), here], x
                    )
        outgoing(i).start()
    for i in range(chunks):
        outgoing(i).wait()


def ocean_call(temp, currents, mixing, flux, edges, land, block_rows, block_cols):
    levels, rows, cols = temp.shape
    chunk = min(32, block_rows)
    anywhere = pl.BlockSpec(memory_space=pl.ANY)
    inside = pl.BlockSpec(memory_space=pltpu.VMEM)
    return pl.pallas_call(
        functools.partial(ocean_kernel, block_rows, block_cols, chunk),
        out_shape=jax.ShapeDtypeStruct(temp.shape, jnp.float32),
        in_specs=[anywhere] * 4 + [inside] * 5 + [pl.BlockSpec(memory_space=pltpu.SMEM)],
        out_specs=anywhere,
        scratch_shapes=[
            pltpu.VMEM((levels, rows + 2 * SUBS, cols), jnp.float32),
            pltpu.VMEM(currents.shape, jnp.float32),
            pltpu.VMEM(mixing.shape, jnp.float32),
            pltpu.VMEM(flux.shape, jnp.float32),
            pltpu.VMEM(temp.shape, jnp.float32),
            pltpu.SemaphoreType.DMA((4, rows // chunk)),
            pltpu.SemaphoreType.DMA((rows // chunk,)),
        ],
        cost_estimate=pl.CostEstimate(
            flops=45 * levels * rows * cols,
            bytes_accessed=5 * 4 * levels * rows * cols,
            transcendentals=levels * rows * cols,
        ),
        compiler_params=pltpu.CompilerParams(vmem_limit_bytes=56 * 2**20),
        name="ocean_column",
    )(temp, currents, mixing, flux, *edges, land)


def shards(temp, currents, mixing, ice_vel, strength, ice_list, land):
    levels, rows, cols = temp.shape
    lon_count = lax.axis_size("lon")
    block_rows = 2 * rows // lon_count
    block_cols = cols // 2
    edges = edges_call(temp)
    vel_out, flux = ice_step_call(
        ice_vel, strength, currents, temp, ice_list, block_rows, block_cols
    )
    temp_out = ocean_call(
        temp,
        currents,
        mixing,
        flux,
        edges,
        land,
        block_rows,
        block_cols,
    )
    return (temp_out, vel_out)


def solution(mesh):
    placed = (
        P(None, "lat", "lon"),
        P(None, None, "lat", "lon"),
        P(None, "lat", "lon"),
        P(None, "lat", "lon"),
        P("lat", "lon"),
        P("lat", "lon", None),
        P("lat", "lon"),
    )
    return jax.shard_map(
        shards,
        mesh=mesh,
        in_specs=placed,
        out_specs=(P(None, "lat", "lon"), P(None, "lat", "lon")),
        check_vma=False,
    )
```
